32 devices in a mesh: row: 8 (over y, x, core), col: 4 (over z).
Axes of the slice: x: 2, y: 2, z: 4, core: 2. Of those that a mesh axis runs over, the one named last changes fastest.
Arguments:
- positions: float32 [3, 65536], P(None, ('row', 'col')), as said below
- species: int32 [65536], P(('row', 'col')), may hold values from 0 to 1
- destination: int32 [2, 65536], P(None, ('row', 'col')), may hold values from 0 to 2047, as said below
- pair_tiles: int32 [8, 4, 2, 384], P('row', 'col'), may hold values from -1 to 127, as said below
Outputs:
- forces: float32 [4, 65536], P(None, ('row', 'col'))
The draws below stay inside these ranges and needn't reach their ends.
Inputs may be any that keep to these rules, and one draw needn't show every extreme that they name: Arriving atoms of device d (the d-th block of 2048 along the arrival order) have destination[0] = o and destination[1] = d * 64 + k with 0 <= k < 64: exactly 64 to every owner o; no two atoms share both entries. `pair_tiles`: entry 0 of a pair is a first-side tile (below 4 * 16), entry 1 a second-side tile (below 8 * 16), or both -1 for an empty entry; an unordered pair of tiles is listed once at most over all blocks; empty entries may stand anywhere. `positions`: atoms sit on a simple cubic lattice of spacing 2.95, each displaced by at most 0.5 per component.
All inputs are finite; a program needn't handle non-finite values.
Results may differ from the reference program's by a relative error of at most 0.0003.
Values sent between devices are 32-bit elements; how exact they have to be, the bound alone decides.
A program may use at most 64 MiB of HBM per device.

```python
import math
import jax
import jax.numpy as jnp
from jax import lax

ATOM_DEV = 2048
TILE = 128
TPD = 16
CAP = 64
PAIRS = 384
ATOMS = 65536
N_ROW = 8
N_COL = 4


def layout_plan(key):
    owners = N_ROW * N_COL
    owner_slot = jax.random.permutation(jax.random.fold_in(key, 11), owners).astype(jnp.int32)
    keys = jax.random.split(jax.random.fold_in(key, 12), owners)
    orders = jax.vmap(lambda one: jax.random.permutation(one, ATOM_DEV))(keys).astype(jnp.int32)
    source = jnp.arange(owners, dtype=jnp.int32)[:, None]
    target = orders // CAP
    within = orders % CAP
    place = source * CAP + within
    return (owner_slot, target.reshape(ATOMS), place.reshape(ATOMS))


def draw_destination(key, part):
    owner_slot, target, place = layout_plan(key)
    return jnp.stack([target, place], 0).astype(jnp.int32)


def draw_positions(key, part):
    owner_slot, target, place = layout_plan(key)
    owner = target
    local = place
    tile = local // TILE
    inner = local % TILE
    slot = owner_slot[owner]
    cell_x = 4 * (slot // N_COL) + inner % 4
    cell_y = 4 * (slot % N_COL) + inner // 4 % 4
    cell_z = 8 * tile + inner // 16
    cells = jnp.stack([cell_x, cell_y, cell_z], 0).astype(jnp.float32)
    jitter = jax.random.uniform(jax.random.fold_in(key, 13), (3, ATOMS), jnp.float32, -0.5, 0.5)
    return (cells + 0.5) * 2.95 + jitter


def draw_pair_tiles(key, part):
    owner_slot, target, place = layout_plan(key)
    first_count = N_COL * TPD
    second_count = N_ROW * TPD
    first = jnp.arange(first_count, dtype=jnp.int32)
    second = jnp.arange(second_count, dtype=jnp.int32)

    def one_block(blk_i, blk_j, sub):
        own_a = blk_i * N_COL + first // TPD
        own_b = second // TPD * N_COL + blk_j
        glob_a = own_a * TPD + first % TPD
        glob_b = own_b * TPD + second % TPD
        slot_a = owner_slot[own_a]
        slot_b = owner_slot[own_b]
        gap_x = jnp.abs(slot_a[:, None] // N_COL - slot_b[None, :] // N_COL)
        gap_x = jnp.minimum(gap_x, N_ROW - gap_x)
        gap_y = jnp.abs(slot_a[:, None] % N_COL - slot_b[None, :] % N_COL)
        gap_y = jnp.minimum(gap_y, N_COL - gap_y)
        gap_z = jnp.abs((first % TPD)[:, None] - (second % TPD)[None, :])
        gap_z = jnp.minimum(gap_z, TPD - gap_z)
        near = (gap_x <= 1) & (gap_y <= 1) & (gap_z <= 1)
        ga = glob_a[:, None]
        gb = glob_b[None, :]
        allowed = near & ((ga == gb) | ((ga < gb) != ((ga + gb) % 2 == 1)))
        flat_allowed = allowed.reshape(-1)
        count = first_count * second_count
        noise = jax.random.randint(sub, (count,), 0, 4096, jnp.int32)
        score = (noise + jnp.where(flat_allowed, 0, 4096)) * count + jnp.arange(count, dtype=jnp.int32)
        picked = jnp.argsort(score)[:PAIRS].astype(jnp.int32)
        keep = flat_allowed[picked] & (noise[picked] % 2 == 0)
        first_pick = jnp.where(keep, picked // second_count, -1)
        second_pick = jnp.where(keep, picked % second_count, -1)
        return jnp.stack([first_pick, second_pick], 0)
    rows = jnp.repeat(jnp.arange(N_ROW, dtype=jnp.int32), N_COL)
    cols = jnp.tile(jnp.arange(N_COL, dtype=jnp.int32), N_ROW)
    subs = jax.random.split(jax.random.fold_in(key, 14), N_ROW * N_COL)
    lists = jax.vmap(one_block)(rows, cols, subs)
    return lists.reshape(N_ROW, N_COL, 2, PAIRS)


def set_ends(result, rng, smallest, high):
    longest = result.shape.index(max(result.shape))
    spots = []
    for shift in (0, 1):
        where = [jax.random.randint(jax.random.fold_in(rng, axis), (), 0, length) for axis, length in enumerate(result.shape)]
        where[longest] = (where[longest] + shift) % result.shape[longest]
        spots.append(tuple(where))
    return result.at[spots[0]].set(smallest).at[spots[1]].set(high)


def setup_inputs(seed: int = 0) -> dict:
    splits = jax.random.split(jax.random.key(seed), 5)
    positions = draw_positions(jax.random.fold_in(splits[4], 71), 0)
    species = set_ends(jax.random.randint(splits[1], (ATOMS,), 0, 2), jax.random.fold_in(splits[1], 1), 0, 1).astype(jnp.int32)
    destination = draw_destination(jax.random.fold_in(splits[4], 71), 0)
    pair_tiles = draw_pair_tiles(jax.random.fold_in(splits[4], 71), 0)
    return dict(positions=positions, species=species, destination=destination, pair_tiles=pair_tiles)


alpha_damp = 0.2
cutoff = 12.0
coulomb = 14.399645
lattice = 2.95
two_over_root = 2.0 / math.sqrt(math.pi)

def pair_terms(dist, charge_prod, amp, decay, disp):
    inv = 1.0 / dist
    inv_six = (inv * inv) ** 3
    screen = jax.scipy.special.erfc(alpha_damp * dist)
    repulse = amp * jnp.exp(-dist / decay)
    energy = coulomb * charge_prod * screen * inv + repulse - disp * inv_six
    force = coulomb * charge_prod * (screen * inv * inv + two_over_root * alpha_damp * jnp.exp(-(alpha_damp * dist) ** 2) * inv) + repulse / decay - 6.0 * disp * inv_six * inv
    return (force, energy)

def interact(row_tiles, col_tiles, weight, same_tile, box):
    diffs = []
    dist_sq = jnp.float32(0.0)
    for comp in range(3):
        delta = row_tiles[comp][:, :, None] - col_tiles[comp][:, None, :]
        delta = delta - box[comp] * jnp.floor(delta / box[comp] + 0.5)
        diffs.append(delta)
        dist_sq = dist_sq + delta * delta
    width = row_tiles.shape[2]
    diagonal = jnp.arange(width)[:, None] == jnp.arange(width)[None, :]
    self_atom = same_tile[:, None, None] & diagonal[None]
    inside = (dist_sq < cutoff * cutoff) & jnp.logical_not(self_atom)
    dist = jnp.sqrt(jnp.where(inside, dist_sq, cutoff * cutoff))
    spec_a = row_tiles[3][:, :, None]
    spec_b = col_tiles[3][:, None, :]
    both_na = (1.0 - spec_a) * (1.0 - spec_b)
    both_cl = spec_a * spec_b
    mixed = 1.0 - both_na - both_cl
    amp = 7895.4 * both_na + 2314.7 * mixed + 1227.2 * both_cl
    decay = 0.1709 * both_na + 0.2903 * mixed + 0.3214 * both_cl
    disp = 29.06 * both_na + 3.47 * both_cl
    charge_prod = (1.0 - 2.0 * spec_a) * (1.0 - 2.0 * spec_b)
    force, energy = pair_terms(dist, charge_prod, amp, decay, disp)
    edge_force, edge_energy = pair_terms(jnp.float32(cutoff), charge_prod, amp, decay, disp)
    shifted_force = force - edge_force
    shifted_energy = energy - edge_energy + (dist - cutoff) * edge_force
    scale = jnp.where(inside, weight[:, None, None], 0.0)
    over_r = scale * shifted_force / dist
    half_energy = 0.5 * scale * shifted_energy
    row_out = jnp.stack([lax.optimization_barrier(jnp.sum(over_r * diffs[0], 2)), lax.optimization_barrier(jnp.sum(over_r * diffs[1], 2)), lax.optimization_barrier(jnp.sum(over_r * diffs[2], 2)), lax.optimization_barrier(jnp.sum(half_energy, 2))], 0)
    col_out = jnp.stack([-lax.optimization_barrier(jnp.sum(over_r * diffs[0], 1)), -lax.optimization_barrier(jnp.sum(over_r * diffs[1], 1)), -lax.optimization_barrier(jnp.sum(over_r * diffs[2], 1)), lax.optimization_barrier(jnp.sum(half_energy, 1))], 0)
    return (row_out, col_out)

def reference(positions, species, destination, pair_tiles):
    payload = jnp.concatenate([positions, species[None].astype(jnp.float32)], 0)
    flat_place = (destination[0] * ATOM_DEV + destination[1]).astype(jnp.int32)
    ordered = jnp.zeros((4, ATOMS), jnp.float32).at[:, flat_place].set(payload)
    owned = ordered.reshape(4, N_ROW, N_COL, TPD, TILE)
    box = (4 * lattice * N_ROW, 4 * lattice * N_COL, 8 * lattice * TPD)
    total = jnp.zeros((4, N_ROW, N_COL, TPD, TILE), jnp.float32)

    def device_step(index, total):
        blk_i = index // N_COL
        blk_j = index % N_COL
        row_block = lax.dynamic_index_in_dim(owned, blk_i, 1, keepdims=False).reshape(4, N_COL * TPD, TILE)
        col_block = lax.dynamic_index_in_dim(owned, blk_j, 2, keepdims=False).reshape(4, N_ROW * TPD, TILE)
        pairs = pair_tiles[blk_i, blk_j]
        blocks = pairs.reshape(2, PAIRS // 16, 16).transpose(1, 0, 2)

        def pair_step(carry, entry):
            row_part, col_part = carry
            first = entry[0]
            second = entry[1]
            valid = first >= 0
            first_safe = jnp.maximum(first, 0)
            second_safe = jnp.maximum(second, 0)
            same_tile = (first_safe // TPD == blk_j) & (second_safe // TPD == blk_i) & (first_safe % TPD == second_safe % TPD)
            weight = jnp.where(valid, jnp.where(same_tile, 0.5, 1.0), 0.0).astype(jnp.float32)
            row_out, col_out = interact(row_block[:, first_safe], col_block[:, second_safe], weight, same_tile, box)
            return ((row_part.at[:, first_safe].add(row_out), col_part.at[:, second_safe].add(col_out)), None)
        start = (jnp.zeros((4, N_COL * TPD, TILE), jnp.float32), jnp.zeros((4, N_ROW * TPD, TILE), jnp.float32))
        (row_part, col_part), unused = lax.scan(pair_step, start, blocks)
        total = total.at[:, blk_i].add(row_part.reshape(4, N_COL, TPD, TILE))
        total = total.at[:, :, blk_j].add(col_part.reshape(4, N_ROW, TPD, TILE))
        return total
    total = lax.fori_loop(0, N_ROW * N_COL, device_step, total)
    return total.reshape(4, ATOMS)
```

```python
import functools
import math

import numpy as np
import jax
import jax.numpy as jnp
from jax import lax
from jax.experimental import pallas as pl
from jax.experimental.pallas import tpu as pltpu
from jax.sharding import PartitionSpec as P

TILE = 128
LANES = 128
HALF = 64
CHUNK = 16
MESH = pl.DeviceIdType.MESH

alpha_damp = 0.2
cutoff = 12.0
coulomb = 14.399645
lattice = 2.95
two_over_root = 2.0 / math.sqrt(math.pi)
LOG2E = 1.0 / math.log(2.0)


def fit_screen(degree):
    nodes = np.cos((np.arange(400) + 0.5) * np.pi / 400)
    r = np.sqrt((nodes + 1.0) * 0.5) * cutoff
    vals = np.array([math.erf(alpha_damp * x) / x for x in r])
    return np.polynomial.chebyshev.cheb2poly(np.polynomial.chebyshev.chebfit(nodes, vals, degree))


SCREEN = [float(c) for c in fit_screen(10)]


def kind_constants(amp, decay, disp, sign):
    rc = cutoff
    x = alpha_damp * rc
    qq = coulomb * sign
    rep = amp * math.exp(-rc / decay)
    f = (
        qq * (math.erfc(x) / rc**2 + two_over_root * alpha_damp * math.exp(-x * x) / rc)
        + rep / decay
        - 6.0 * disp / rc**7
    )
    u = qq * math.erfc(x) / rc + rep - disp / rc**6
    return dict(
        qq=qq, lead=math.log2(amp), rate=LOG2E / decay, disp=disp, edge=f, base=-u - rc * f
    )


KINDS = [
    kind_constants(7895.4, 0.1709, 29.06, 1.0),
    kind_constants(2314.7, 0.2903, 0.0, -1.0),
    kind_constants(1227.2, 0.3214, 3.47, 1.0),
]
NAMES = ("lead", "rate", "disp", "edge", "base")


def pair_kernel(box, tiles_dev, a_ref, b_ref, pairs_ref, row_ref, col_ref, at_ref, acc_ref, cacc_ref, mi_ref, mf_ref, si_ref, sf_ref, sems):
    blk_i = lax.axis_index("row")
    blk_j = lax.axis_index("col")
    n_first = a_ref.shape[1]
    n_second = b_ref.shape[1]
    entries = pairs_ref.shape[1]
    hi = lax.Precision.HIGHEST
    p = pairs_ref[0:1, :]
    q = pairs_ref[1:2, :]
    pick_a = (lax.broadcasted_iota(jnp.int32, (n_first, entries), 0) == p).astype(jnp.float32)
    pick_b = (lax.broadcasted_iota(jnp.int32, (n_second, entries), 0) == q).astype(jnp.float32)
    tab_a = []
    tab_b = []
    for c in range(4):
        at = a_ref[c].T
        for k in range(at_ref.shape[1]):
            width = min(LANES, n_first - k * LANES)
            at_ref[c, k, :, :width] = at[:, k * LANES : k * LANES + width]
        if c < 3:
            for h in range(2):
                part = at[h * HALF : (h + 1) * HALF]
                tab_a.append(jnp.min(part, 0, keepdims=True))
                tab_a.append(jnp.max(part, 0, keepdims=True))
            bt = b_ref[c].T
            tab_b.append(jnp.min(bt, 0, keepdims=True))
            tab_b.append(jnp.max(bt, 0, keepdims=True))
    fill_a = [jnp.zeros((1, n_first), jnp.float32)] * 4
    fill_b = [jnp.zeros((1, n_second), jnp.float32)] * 2
    got_a = jnp.dot(jnp.concatenate(tab_a + fill_a, 0), pick_a, precision=hi, preferred_element_type=jnp.float32)
    got_b = jnp.dot(jnp.concatenate(tab_b + fill_b, 0), pick_b, precision=hi, preferred_element_type=jnp.float32)
    gaps = [0.0, 0.0]
    plain = p >= 0
    shifts = []
    for c in range(3):
        lows = [got_a[4 * c : 4 * c + 1], got_a[4 * c + 2 : 4 * c + 3]]
        highs = [got_a[4 * c + 1 : 4 * c + 2], got_a[4 * c + 3 : 4 * c + 4]]
        low = jnp.minimum(lows[0], lows[1])
        high = jnp.maximum(highs[0], highs[1])
        blow = got_b[2 * c : 2 * c + 1]
        bhigh = got_b[2 * c + 1 : 2 * c + 2]
        shift = box[c] * jnp.floor(0.5 * (low + high - blow - bhigh) / box[c] + 0.5)
        shifts.append(shift)
        blow = blow + shift
        bhigh = bhigh + shift
        reach = jnp.maximum(high - blow, bhigh - low)
        plain = plain & (reach <= box[c] - cutoff - 0.05)
        for h in range(2):
            gap = jnp.maximum(jnp.maximum(lows[h] - bhigh, blow - highs[h]) - 0.01, 0.0)
            gaps[h] = gaps[h] + gap * gap
    near = [(g < cutoff * cutoff).astype(jnp.int32) for g in gaps]
    same = (p // tiles_dev == blk_j) & (q // tiles_dev == blk_i) & (p % tiles_dev == q % tiles_dev)
    simple = plain & jnp.logical_not(same)
    mode = jnp.where(simple, near[0] + 2 * near[1], jnp.where(same, 8, 4))
    mode = jnp.where(p >= 0, mode, 0)
    mi_ref[0:1, :] = p
    mi_ref[1:2, :] = q
    mi_ref[2:3, :] = mode
    for c in range(3):
        mf_ref[c : c + 1, :] = shifts[c]
    one = pltpu.make_async_copy(mi_ref, si_ref, sems.at[0])
    two = pltpu.make_async_copy(mf_ref, sf_ref, sems.at[1])
    one.start()
    two.start()
    acc_ref[...] = jnp.zeros_like(acc_ref)
    cacc_ref[...] = jnp.zeros_like(cacc_ref)
    one.wait()
    two.wait()
    lane = lax.broadcasted_iota(jnp.int32, (CHUNK, LANES), 1)
    sub = lax.broadcasted_iota(jnp.int32, (CHUNK, LANES), 0)

    def work(e, half, general):
        first = si_ref[0, e]
        second = si_ref[1, e]
        bank = first // LANES
        spot = first % LANES
        turn = (LANES - spot) % LANES
        rows = [b_ref[c, pl.ds(second, 1), :] for c in range(4)]
        if general:
            mode_now = si_ref[2, e]
            is_same = mode_now >= 8
            weight = jnp.where(is_same, 0.5, 1.0).astype(jnp.float32)
        else:
            for c in range(3):
                rows[c] = rows[c] + sf_ref[c, e]
        spec_b = rows[3] > 0.5
        light = {n: jnp.broadcast_to(jnp.where(spec_b, KINDS[1][n], KINDS[0][n]), (CHUNK, LANES)) for n in NAMES}
        heavy = {n: jnp.broadcast_to(jnp.where(spec_b, KINDS[2][n], KINDS[1][n]), (CHUNK, LANES)) for n in NAMES}
        charge = jnp.broadcast_to(coulomb * (1.0 - 2.0 * rows[3]), (CHUNK, LANES))
        xyz = [jnp.broadcast_to(rows[c], (CHUNK, LANES)) for c in range(3)]
        sums = [jnp.zeros((8, LANES), jnp.float32) for _ in range(4)]
        mine = lane == spot
        starts = range(0, TILE, CHUNK) if general else range(half * HALF, half * HALF + HALF, CHUNK)
        for s in starts:
            cols = [pltpu.roll(at_ref[c, bank, s : s + CHUNK, :], turn, 1)[:, 0:1] for c in range(4)]
            d = []
            for c in range(3):
                v = cols[c] - xyz[c]
                if general:
                    v = v - box[c] * jnp.floor(v / box[c] + 0.5)
                d.append(v)
            r2 = d[0] * d[0] + d[1] * d[1] + d[2] * d[2]
            inside = r2 < cutoff * cutoff
            if general:
                inside = inside & jnp.logical_not(is_same & (lane == sub + s))
            inv = lax.rsqrt(r2)
            r = r2 * inv
            inv2 = inv * inv
            u = r2 * (1.0 / 72.0) - 1.0
            poly = jnp.float32(SCREEN[-1]) * u + SCREEN[-2]
            for coef in SCREEN[-3::-1]:
                poly = poly * u + coef
            screen = inv - poly
            gauss = jnp.exp2(r2 * (-(alpha_damp**2) * LOG2E) + math.log2(two_over_root * alpha_damp))
            is_cl = jnp.broadcast_to(cols[3], (CHUNK, LANES)) > 0.5
            k = {n: jnp.where(is_cl, heavy[n], light[n]) for n in NAMES}
            qq = jnp.where(is_cl, -charge, charge)
            rep = jnp.exp2(k["lead"] - r * k["rate"])
            six = k["disp"] * (inv2 * inv2 * inv2)
            energy = qq * screen + rep - six + (r * k["edge"] + k["base"])
            over = inv2 * (qq * (screen + gauss) - 6.0 * six) + inv * (
                rep * (k["rate"] * (1.0 / LOG2E)) - k["edge"]
            )
            over = jnp.where(inside, over, 0.0)
            energy = jnp.where(inside, energy, 0.0)
            terms = [over * d[0], over * d[1], over * d[2], energy]
            for c in range(4):
                t = terms[c]
                for m in range(0, CHUNK, 8):
                    sums[c] = sums[c] + t[m : m + 8]
                red = jnp.sum(t, 1, keepdims=True)
                if general:
                    red = red * weight
                acc_ref[c, bank, s : s + CHUNK, :] += jnp.where(mine, red, 0.0)
        for c in range(4):
            v = sums[c]
            if general:
                v = v * weight
            cacc_ref[c, second] += v

    def turn_pair(e, carry):
        mode = si_ref[2, e]
        for half in range(2):
            @pl.when((mode == 1 + half) | (mode == 3))
            def _():
                work(e, half, False)

        @pl.when(mode >= 4)
        def _():
            work(e, 0, True)

        return carry

    lax.fori_loop(0, entries, turn_pair, 0)
    for c in range(4):
        scale = 0.5 if c == 3 else 1.0
        for k in range(at_ref.shape[1]):
            width = min(LANES, n_first - k * LANES)
            row_ref[c, k * LANES : k * LANES + width, :] = scale * acc_ref[c, k].T[:width]
        col_ref[c] = jnp.sum(cacc_ref[c], 1) * (0.5 if c == 3 else -1.0)


def reduce_kernel(n_row, n_col, row_ref, col_ref, out_ref, row_got, col_got, send_a, recv_a, send_b, recv_b):
    blk_i = lax.axis_index("row")
    blk_j = lax.axis_index("col")
    tiles = out_ref.shape[1]
    barrier = pltpu.get_barrier_semaphore()
    for k in range(1, n_row):
        pl.semaphore_signal(barrier, inc=1, device_id=(lax.rem(blk_i + k, n_row), blk_j), device_id_type=MESH)
    for k in range(1, n_col):
        pl.semaphore_signal(barrier, inc=1, device_id=(blk_i, lax.rem(blk_j + k, n_col)), device_id_type=MESH)
    pl.semaphore_wait(barrier, n_row + n_col - 2)
    copies = []
    for k in range(1, n_row):
        to = lax.rem(blk_i + k, n_row)
        copies.append(
            pltpu.make_async_remote_copy(
                src_ref=col_ref.at[:, pl.ds(pl.multiple_of(to * tiles, tiles), tiles), :],
                dst_ref=col_got.at[k - 1],
                send_sem=send_b.at[k - 1],
                recv_sem=recv_b.at[k - 1],
                device_id=(to, blk_j),
                device_id_type=MESH,
            )
        )
        copies[-1].start()
    for k in range(1, n_col):
        to = lax.rem(blk_j + k, n_col)
        copies.append(
            pltpu.make_async_remote_copy(
                src_ref=row_ref.at[:, pl.ds(pl.multiple_of(to * tiles, tiles), tiles), :],
                dst_ref=row_got.at[k - 1],
                send_sem=send_a.at[k - 1],
                recv_sem=recv_a.at[k - 1],
                device_id=(blk_i, to),
                device_id_type=MESH,
            )
        )
        copies[-1].start()
    total = row_ref[:, pl.ds(pl.multiple_of(blk_j * tiles, tiles), tiles), :] + col_ref[:, pl.ds(pl.multiple_of(blk_i * tiles, tiles), tiles), :]
    for copy in copies:
        copy.wait()
    for k in range(n_row - 1):
        total = total + col_got[k]
    for k in range(n_col - 1):
        total = total + row_got[k]
    out_ref[...] = total


def local(positions, species, destination, pair_tiles):
    n_row = lax.axis_size("row")
    n_col = lax.axis_size("col")
    atom_dev = positions.shape[1]
    owners = n_row * n_col
    capacity = atom_dev // owners
    tiles_dev = atom_dev // TILE
    payload = jnp.concatenate([positions, species[None].astype(jnp.float32)], 0)
    target = destination[0]
    slot_index = target * capacity + destination[1] % capacity
    outgoing = jnp.zeros((4, owners * capacity), jnp.float32).at[:, slot_index].set(payload)
    outgoing = outgoing.reshape(4, n_row, n_col, capacity)
    arrived = lax.all_to_all(
        lax.all_to_all(outgoing, "row", split_axis=1, concat_axis=1, tiled=True),
        "col",
        split_axis=2,
        concat_axis=2,
        tiled=True,
    )
    owned = arrived.reshape(4, tiles_dev, TILE)
    row_block = lax.all_gather(owned, "col", axis=1, tiled=True)
    col_block = lax.all_gather(owned, "row", axis=1, tiled=True)
    n_first = row_block.shape[1]
    n_second = col_block.shape[1]
    box = (4 * lattice * n_row, 4 * lattice * n_col, 8 * lattice * tiles_dev)
    entries = pair_tiles.shape[3]
    lists = pair_tiles.reshape(2, entries)
    banks = -(-n_first // LANES)
    vmem = pl.BlockSpec(memory_space=pltpu.VMEM)
    row_part, col_part = pl.pallas_call(
        functools.partial(pair_kernel, box, tiles_dev),
        out_shape=(
            jax.ShapeDtypeStruct((4, n_first, TILE), jnp.float32),
            jax.ShapeDtypeStruct((4, n_second, TILE), jnp.float32),
        ),
        in_specs=[vmem] * 3,
        out_specs=(vmem, vmem),
        scratch_shapes=[
            pltpu.VMEM((4, banks, TILE, LANES), jnp.float32),
            pltpu.VMEM((4, banks, TILE, LANES), jnp.float32),
            pltpu.VMEM((4, n_second, 8, LANES), jnp.float32),
            pltpu.VMEM((8, entries), jnp.int32),
            pltpu.VMEM((8, entries), jnp.float32),
            pltpu.SMEM((8, entries), jnp.int32),
            pltpu.SMEM((8, entries), jnp.float32),
            pltpu.SemaphoreType.DMA((2,)),
        ],
        compiler_params=pltpu.CompilerParams(vmem_limit_bytes=48 * 1024 * 1024),
        name="pairs",
    )(row_block, col_block, lists)
    out = pl.pallas_call(
        functools.partial(reduce_kernel, n_row, n_col),
        out_shape=jax.ShapeDtypeStruct((4, tiles_dev, TILE), jnp.float32),
        in_specs=[vmem] * 2,
        out_specs=vmem,
        scratch_shapes=[
            pltpu.VMEM((n_col - 1, 4, tiles_dev, TILE), jnp.float32),
            pltpu.VMEM((n_row - 1, 4, tiles_dev, TILE), jnp.float32),
            pltpu.SemaphoreType.DMA((n_col - 1,)),
            pltpu.SemaphoreType.DMA((n_col - 1,)),
            pltpu.SemaphoreType.DMA((n_row - 1,)),
            pltpu.SemaphoreType.DMA((n_row - 1,)),
        ],
        compiler_params=pltpu.CompilerParams(
            collective_id=0, has_side_effects=True, vmem_limit_bytes=32 * 1024 * 1024
        ),
        name="reduce",
    )(row_part, col_part)
    return out.reshape(4, atom_dev)


def solution(mesh):
    return jax.shard_map(
        local,
        mesh=mesh,
        in_specs=(
            P(None, ("row", "col")),
            P(("row", "col")),
            P(None, ("row", "col")),
            P("row", "col", None, None),
        ),
        out_specs=P(None, ("row", "col")),
        check_vma=False,
    )
```

```python
import functools
import math

import numpy as np
import jax
import jax.numpy as jnp
from jax import lax
from jax.experimental import pallas as pl
from jax.experimental.pallas import tpu as pltpu
from jax.sharding import PartitionSpec as P

TILE = 128
LANES = 128
HALF = 64
CHUNK = 16
MESH = pl.DeviceIdType.MESH

alpha_damp = 0.2
cutoff = 12.0
coulomb = 14.399645
lattice = 2.95
two_over_root = 2.0 / math.sqrt(math.pi)
LOG2E = 1.0 / math.log(2.0)


def fit_screen(degree):
    nodes = np.cos((np.arange(400) + 0.5) * np.pi / 400)
    r = np.sqrt((nodes + 1.0) * 0.5) * cutoff
    vals = np.array([math.erf(alpha_damp * x) / x for x in r])
    return np.polynomial.chebyshev.cheb2poly(np.polynomial.chebyshev.chebfit(nodes, vals, degree))


SCREEN = [float(c) for c in fit_screen(10)]


def kind_constants(amp, decay, disp, sign):
    rc = cutoff
    x = alpha_damp * rc
    qq = coulomb * sign
    rep = amp * math.exp(-rc / decay)
    f = (
        qq * (math.erfc(x) / rc**2 + two_over_root * alpha_damp * math.exp(-x * x) / rc)
        + rep / decay
        - 6.0 * disp / rc**7
    )
    u = qq * math.erfc(x) / rc + rep - disp / rc**6
    return dict(
        qq=qq, lead=math.log2(amp), rate=LOG2E / decay, disp=disp, edge=f, base=-u - rc * f
    )


KINDS = [
    kind_constants(7895.4, 0.1709, 29.06, 1.0),
    kind_constants(2314.7, 0.2903, 0.0, -1.0),
    kind_constants(1227.2, 0.3214, 3.47, 1.0),
]
NAMES = ("lead", "rate", "disp", "edge", "base")


def pair_kernel(box, tiles_dev, a_ref, b_ref, pairs_ref, row_ref, col_ref, at_ref, acc_ref, cacc_ref, mi_ref, mf_ref, si_ref, sf_ref, sems):
    blk_i = lax.axis_index("row")
    blk_j = lax.axis_index("col")
    n_first = a_ref.shape[1]
    n_second = b_ref.shape[1]
    entries = pairs_ref.shape[1]
    hi = lax.Precision.HIGHEST
    p = pairs_ref[0:1, :]
    q = pairs_ref[1:2, :]
    pick_a = (lax.broadcasted_iota(jnp.int32, (n_first, entries), 0) == p).astype(jnp.float32)
    pick_b = (lax.broadcasted_iota(jnp.int32, (n_second, entries), 0) == q).astype(jnp.float32)
    tab_a = []
    tab_b = []
    for c in range(4):
        at = a_ref[c].T
        for k in range(at_ref.shape[1]):
            width = min(LANES, n_first - k * LANES)
            at_ref[c, k, :, :width] = at[:, k * LANES : k * LANES + width]
        if c < 3:
            for h in range(2):
                part = at[h * HALF : (h + 1) * HALF]
                tab_a.append(jnp.min(part, 0, keepdims=True))
                tab_a.append(jnp.max(part, 0, keepdims=True))
            bt = b_ref[c].T
            tab_b.append(jnp.min(bt, 0, keepdims=True))
            tab_b.append(jnp.max(bt, 0, keepdims=True))
    fill_a = [jnp.zeros((1, n_first), jnp.float32)] * 4
    fill_b = [jnp.zeros((1, n_second), jnp.float32)] * 2
    got_a = jnp.dot(jnp.concatenate(tab_a + fill_a, 0), pick_a, precision=hi, preferred_element_type=jnp.float32)
    got_b = jnp.dot(jnp.concatenate(tab_b + fill_b, 0), pick_b, precision=hi, preferred_element_type=jnp.float32)
    gaps = [0.0, 0.0]
    plain = p >= 0
    shifts = []
    for c in range(3):
        lows = [got_a[4 * c : 4 * c + 1], got_a[4 * c + 2 : 4 * c + 3]]
        highs = [got_a[4 * c + 1 : 4 * c + 2], got_a[4 * c + 3 : 4 * c + 4]]
        low = jnp.minimum(lows[0], lows[1])
        high = jnp.maximum(highs[0], highs[1])
        blow = got_b[2 * c : 2 * c + 1]
        bhigh = got_b[2 * c + 1 : 2 * c + 2]
        shift = box[c] * jnp.floor(0.5 * (low + high - blow - bhigh) / box[c] + 0.5)
        shifts.append(shift)
        blow = blow + shift
        bhigh = bhigh + shift
        reach = jnp.maximum(high - blow, bhigh - low)
        plain = plain & (reach <= box[c] - cutoff - 0.05)
        for h in range(2):
            gap = jnp.maximum(jnp.maximum(lows[h] - bhigh, blow - highs[h]) - 0.01, 0.0)
            gaps[h] = gaps[h] + gap * gap
    near = [(g < cutoff * cutoff).astype(jnp.int32) for g in gaps]
    same = (p // tiles_dev == blk_j) & (q // tiles_dev == blk_i) & (p % tiles_dev == q % tiles_dev)
    simple = plain & jnp.logical_not(same)
    mode = jnp.where(simple, near[0] + 2 * near[1], jnp.where(same, 8, 4))
    mode = jnp.where(p >= 0, mode, 0)
    mi_ref[0:1, :] = p
    mi_ref[1:2, :] = q
    mi_ref[2:3, :] = mode
    for c in range(3):
        mf_ref[c : c + 1, :] = shifts[c]
    one = pltpu.make_async_copy(mi_ref, si_ref, sems.at[0])
    two = pltpu.make_async_copy(mf_ref, sf_ref, sems.at[1])
    one.start()
    two.start()
    acc_ref[...] = jnp.zeros_like(acc_ref)
    cacc_ref[...] = jnp.zeros_like(cacc_ref)
    one.wait()
    two.wait()
    lane = lax.broadcasted_iota(jnp.int32, (CHUNK, LANES), 1)
    sub = lax.broadcasted_iota(jnp.int32, (CHUNK, LANES), 0)

    def work(e, half, general):
        first = si_ref[0, e]
        second = si_ref[1, e]
        bank = first // LANES
        spot = first % LANES
        turn = (LANES - spot) % LANES
        rows = [b_ref[c, pl.ds(second, 1), :] for c in range(4)]
        if general:
            mode_now = si_ref[2, e]
            is_same = mode_now >= 8
            weight = jnp.where(is_same, 0.5, 1.0).astype(jnp.float32)
        else:
            for c in range(3):
                rows[c] = rows[c] + sf_ref[c, e]
        spec_b = rows[3] > 0.5
        light = {n: jnp.broadcast_to(jnp.where(spec_b, KINDS[1][n], KINDS[0][n]), (CHUNK, LANES)) for n in NAMES}
        heavy = {n: jnp.broadcast_to(jnp.where(spec_b, KINDS[2][n], KINDS[1][n]), (CHUNK, LANES)) for n in NAMES}
        charge = jnp.broadcast_to(coulomb * (1.0 - 2.0 * rows[3]), (CHUNK, LANES))
        xyz = [jnp.broadcast_to(rows[c], (CHUNK, LANES)) for c in range(3)]
        sums = [jnp.zeros((8, LANES), jnp.float32) for _ in range(4)]
        mine = lane == spot
        starts = range(0, TILE, CHUNK) if general else range(half * HALF, half * HALF + HALF, CHUNK)
        for s in starts:
            cols = [pltpu.roll(at_ref[c, bank, s : s + CHUNK, :], turn, 1)[:, 0:1] for c in range(4)]
            d = []
            for c in range(3):
                v = cols[c] - xyz[c]
                if general:
                    v = v - box[c] * jnp.floor(v / box[c] + 0.5)
                d.append(v)
            r2 = d[0] * d[0] + d[1] * d[1] + d[2] * d[2]
            inside = r2 < cutoff * cutoff
            if general:
                inside = inside & jnp.logical_not(is_same & (lane == sub + s))
            inv = lax.rsqrt(r2)
            r = r2 * inv
            inv2 = inv * inv
            u = r2 * (1.0 / 72.0) - 1.0
            poly = jnp.float32(SCREEN[-1]) * u + SCREEN[-2]
            for coef in SCREEN[-3::-1]:
                poly = poly * u + coef
            screen = inv - poly
            gauss = jnp.exp2(r2 * (-(alpha_damp**2) * LOG2E) + math.log2(two_over_root * alpha_damp))
            is_cl = jnp.broadcast_to(cols[3], (CHUNK, LANES)) > 0.5
            k = {n: jnp.where(is_cl, heavy[n], light[n]) for n in NAMES}
            qq = jnp.where(is_cl, -charge, charge)
            rep = jnp.exp2(k["lead"] - r * k["rate"])
            six = k["disp"] * (inv2 * inv2 * inv2)
            energy = qq * screen + rep - six + (r * k["edge"] + k["base"])
            over = inv2 * (qq * (screen + gauss) - 6.0 * six) + inv * (
                rep * (k["rate"] * (1.0 / LOG2E)) - k["edge"]
            )
            over = jnp.where(inside, over, 0.0)
            energy = jnp.where(inside, energy, 0.0)
            terms = [over * d[0], over * d[1], over * d[2], energy]
            for c in range(4):
                t = terms[c]
                for m in range(0, CHUNK, 8):
                    sums[c] = sums[c] + t[m : m + 8]
                red = jnp.sum(t, 1, keepdims=True)
                if general:
                    red = red * weight
                acc_ref[c, bank, s : s + CHUNK, :] += jnp.where(mine, red, 0.0)
        for c in range(4):
            v = sums[c]
            if general:
                v = v * weight
            cacc_ref[c, second] += v

    def turn_pair(e, carry):
        mode = si_ref[2, e]
        for half in range(2):
            @pl.when((mode == 1 + half) | (mode == 3))
            def _():
                work(e, half, False)

        @pl.when(mode >= 4)
        def _():
            work(e, 0, True)

        return carry

    lax.fori_loop(0, entries, turn_pair, 0)
    for c in range(4):
        scale = 0.5 if c == 3 else 1.0
        for k in range(at_ref.shape[1]):
            width = min(LANES, n_first - k * LANES)
            row_ref[c, k * LANES : k * LANES + width, :] = scale * acc_ref[c, k].T[:width]
        col_ref[c] = jnp.sum(cacc_ref[c], 1) * (0.5 if c == 3 else -1.0)


def reduce_kernel(n_row, n_col, row_ref, col_ref, out_ref, row_got, col_got, send_a, recv_a, send_b, recv_b):
    blk_i = lax.axis_index("row")
    blk_j = lax.axis_index("col")
    tiles = out_ref.shape[1]
    barrier = pltpu.get_barrier_semaphore()
    for k in range(1, n_row):
        pl.semaphore_signal(barrier, inc=1, device_id=(lax.rem(blk_i + k, n_row), blk_j), device_id_type=MESH)
    for k in range(1, n_col):
        pl.semaphore_signal(barrier, inc=1, device_id=(blk_i, lax.rem(blk_j + k, n_col)), device_id_type=MESH)
    pl.semaphore_wait(barrier, n_row + n_col - 2)
    copies = []
    for k in range(1, n_row):
        to = lax.rem(blk_i + k, n_row)
        copies.append(
            pltpu.make_async_remote_copy(
                src_ref=col_ref.at[:, pl.ds(pl.multiple_of(to * tiles, tiles), tiles), :],
                dst_ref=col_got.at[k - 1],
                send_sem=send_b.at[k - 1],
                recv_sem=recv_b.at[k - 1],
                device_id=(to, blk_j),
                device_id_type=MESH,
            )
        )
        copies[-1].start()
    for k in range(1, n_col):
        to = lax.rem(blk_j + k, n_col)
        copies.append(
            pltpu.make_async_remote_copy(
                src_ref=row_ref.at[:, pl.ds(pl.multiple_of(to * tiles, tiles), tiles), :],
                dst_ref=row_got.at[k - 1],
                send_sem=send_a.at[k - 1],
                recv_sem=recv_a.at[k - 1],
                device_id=(blk_i, to),
                device_id_type=MESH,
            )
        )
        copies[-1].start()
    total = row_ref[:, pl.ds(pl.multiple_of(blk_j * tiles, tiles), tiles), :] + col_ref[:, pl.ds(pl.multiple_of(blk_i * tiles, tiles), tiles), :]
    for copy in copies:
        copy.wait()
    for k in range(n_row - 1):
        total = total + col_got[k]
    for k in range(n_col - 1):
        total = total + row_got[k]
    out_ref[...] = total


def exchange_kernel(n_row, n_col, pos_ref, spec_ref, dest_ref, a_ref, b_ref, outgoing, arrived, owned, send_x, recv_x, send_a, recv_a, send_b, recv_b):
    blk_i = lax.axis_index("row")
    blk_j = lax.axis_index("col")
    owners = n_row * n_col
    me = blk_i * n_col + blk_j
    tiles = owned.shape[1]
    atoms = pos_ref.shape[1]
    capacity = atoms // owners
    ratio = TILE // capacity
    barrier = pltpu.get_barrier_semaphore()

    def coords(k):
        to = lax.rem(me + k, owners)
        return to, (to // n_col, lax.rem(to, n_col))

    def greet(k, carry):
        pl.semaphore_signal(barrier, inc=1, device_id=coords(k)[1], device_id_type=MESH)
        return carry

    lax.fori_loop(1, owners, greet, 0)
    owner_hot = lax.broadcasted_iota(jnp.int32, (owners, atoms), 0) == dest_ref[0:1, :]
    lane = lax.rem(dest_ref[1:2, :], capacity) + lax.rem(me, ratio) * capacity
    lane_hot = (lax.broadcasted_iota(jnp.int32, (TILE, atoms), 0) == lane).astype(jnp.float32).astype(jnp.bfloat16)
    for c in range(4):
        rest = pos_ref[c : c + 1, :] if c < 3 else spec_ref[...].astype(jnp.float32)
        total = None
        for piece in range(3 if c < 3 else 1):
            part = rest.astype(jnp.bfloat16).astype(jnp.float32)
            rest = rest - part
            spread = jnp.where(owner_hot, part, 0.0).astype(jnp.bfloat16)
            got = lax.dot_general(spread, lane_hot, (((1,), (1,)), ((), ())), preferred_element_type=jnp.float32)
            total = got if total is None else total + got
        outgoing[:, c, :] = total
    pl.semaphore_wait(barrier, owners - 1)

    def send(k):
        to, where = coords(k)
        return pltpu.make_async_remote_copy(
            src_ref=outgoing.at[to],
            dst_ref=arrived.at[me],
            send_sem=send_x.at[k - 1],
            recv_sem=recv_x.at[k - 1],
            device_id=where,
            device_id_type=MESH,
        )

    def start(k, carry):
        send(k).start()
        return carry

    def finish(k, carry):
        send(k).wait()
        return carry

    lax.fori_loop(1, owners, start, 0)
    arrived[pl.ds(me, 1)] = outgoing[pl.ds(me, 1)]
    lax.fori_loop(1, owners, finish, 0)
    whole = jnp.sum(arrived[...].reshape(tiles, ratio, 4, TILE), 1)
    for c in range(4):
        owned[c] = whole[:, c, :]
    copies = []
    at_a = pl.ds(pl.multiple_of(blk_j * tiles, tiles), tiles)
    at_b = pl.ds(pl.multiple_of(blk_i * tiles, tiles), tiles)
    for k in range(1, n_row):
        copies.append(
            pltpu.make_async_remote_copy(
                src_ref=owned,
                dst_ref=b_ref.at[:, at_b, :],
                send_sem=send_b.at[k - 1],
                recv_sem=recv_b.at[k - 1],
                device_id=(lax.rem(blk_i + k, n_row), blk_j),
                device_id_type=MESH,
            )
        )
        copies[-1].start()
    for k in range(1, n_col):
        copies.append(
            pltpu.make_async_remote_copy(
                src_ref=owned,
                dst_ref=a_ref.at[:, at_a, :],
                send_sem=send_a.at[k - 1],
                recv_sem=recv_a.at[k - 1],
                device_id=(blk_i, lax.rem(blk_j + k, n_col)),
                device_id_type=MESH,
            )
        )
        copies[-1].start()
    a_ref[:, at_a, :] = owned[...]
    b_ref[:, at_b, :] = owned[...]
    for copy in copies:
        copy.wait()


def local(positions, species, destination, pair_tiles):
    n_row = lax.axis_size("row")
    n_col = lax.axis_size("col")
    atom_dev = positions.shape[1]
    owners = n_row * n_col
    tiles_dev = atom_dev // TILE
    n_first = n_col * tiles_dev
    n_second = n_row * tiles_dev
    vmem = pl.BlockSpec(memory_space=pltpu.VMEM)
    row_block, col_block = pl.pallas_call(
        functools.partial(exchange_kernel, n_row, n_col),
        out_shape=(
            jax.ShapeDtypeStruct((4, n_first, TILE), jnp.float32),
            jax.ShapeDtypeStruct((4, n_second, TILE), jnp.float32),
        ),
        in_specs=[vmem] * 3,
        out_specs=(vmem, vmem),
        scratch_shapes=[
            pltpu.VMEM((owners, 4, TILE), jnp.float32),
            pltpu.VMEM((owners, 4, TILE), jnp.float32),
            pltpu.VMEM((4, tiles_dev, TILE), jnp.float32),
            pltpu.SemaphoreType.DMA((owners - 1,)),
            pltpu.SemaphoreType.DMA((owners - 1,)),
            pltpu.SemaphoreType.DMA((n_col - 1,)),
            pltpu.SemaphoreType.DMA((n_col - 1,)),
            pltpu.SemaphoreType.DMA((n_row - 1,)),
            pltpu.SemaphoreType.DMA((n_row - 1,)),
        ],
        compiler_params=pltpu.CompilerParams(
            collective_id=1, has_side_effects=True, vmem_limit_bytes=40 * 1024 * 1024
        ),
        name="exchange",
    )(positions, species[None], destination)
    box = (4 * lattice * n_row, 4 * lattice * n_col, 8 * lattice * tiles_dev)
    entries = pair_tiles.shape[3]
    lists = pair_tiles.reshape(2, entries)
    banks = -(-n_first // LANES)
    row_part, col_part = pl.pallas_call(
        functools.partial(pair_kernel, box, tiles_dev),
        out_shape=(
            jax.ShapeDtypeStruct((4, n_first, TILE), jnp.float32),
            jax.ShapeDtypeStruct((4, n_second, TILE), jnp.float32),
        ),
        in_specs=[vmem] * 3,
        out_specs=(vmem, vmem),
        scratch_shapes=[
            pltpu.VMEM((4, banks, TILE, LANES), jnp.float32),
            pltpu.VMEM((4, banks, TILE, LANES), jnp.float32),
            pltpu.VMEM((4, n_second, 8, LANES), jnp.float32),
            pltpu.VMEM((8, entries), jnp.int32),
            pltpu.VMEM((8, entries), jnp.float32),
            pltpu.SMEM((8, entries), jnp.int32),
            pltpu.SMEM((8, entries), jnp.float32),
            pltpu.SemaphoreType.DMA((2,)),
        ],
        compiler_params=pltpu.CompilerParams(vmem_limit_bytes=48 * 1024 * 1024),
        name="pairs",
    )(row_block, col_block, lists)
    out = pl.pallas_call(
        functools.partial(reduce_kernel, n_row, n_col),
        out_shape=jax.ShapeDtypeStruct((4, tiles_dev, TILE), jnp.float32),
        in_specs=[vmem] * 2,
        out_specs=vmem,
        scratch_shapes=[
            pltpu.VMEM((n_col - 1, 4, tiles_dev, TILE), jnp.float32),
            pltpu.VMEM((n_row - 1, 4, tiles_dev, TILE), jnp.float32),
            pltpu.SemaphoreType.DMA((n_col - 1,)),
            pltpu.SemaphoreType.DMA((n_col - 1,)),
            pltpu.SemaphoreType.DMA((n_row - 1,)),
            pltpu.SemaphoreType.DMA((n_row - 1,)),
        ],
        compiler_params=pltpu.CompilerParams(
            collective_id=0, has_side_effects=True, vmem_limit_bytes=32 * 1024 * 1024
        ),
        name="reduce",
    )(row_part, col_part)
    return out.reshape(4, atom_dev)


def solution(mesh):
    return jax.shard_map(
        local,
        mesh=mesh,
        in_specs=(
            P(None, ("row", "col")),
            P(("row", "col")),
            P(None, ("row", "col")),
            P("row", "col", None, None),
        ),
        out_specs=P(None, ("row", "col")),
        check_vma=False,
    )
```

```python
import functools
import math

import numpy as np
import jax
import jax.numpy as jnp
from jax import lax
from jax.experimental import pallas as pl
from jax.experimental.pallas import tpu as pltpu
from jax.sharding import PartitionSpec as P

TILE = 128
LANES = 128
HALF = 64
WIDE_TILES = 64
CHUNK = 16
MESH = pl.DeviceIdType.MESH

alpha_damp = 0.2
cutoff = 12.0
coulomb = 14.399645
lattice = 2.95
two_over_root = 2.0 / math.sqrt(math.pi)
LOG2E = 1.0 / math.log(2.0)


def fit_screen(degree):
    nodes = np.cos((np.arange(400) + 0.5) * np.pi / 400)
    r = np.sqrt((nodes + 1.0) * 0.5) * cutoff
    vals = np.array([math.erf(alpha_damp * x) / x for x in r])
    return np.polynomial.chebyshev.cheb2poly(np.polynomial.chebyshev.chebfit(nodes, vals, degree))


SCREEN = [float(c) for c in fit_screen(10)]


def kind_constants(amp, decay, disp, sign):
    rc = cutoff
    x = alpha_damp * rc
    qq = coulomb * sign
    rep = amp * math.exp(-rc / decay)
    f = (
        qq * (math.erfc(x) / rc**2 + two_over_root * alpha_damp * math.exp(-x * x) / rc)
        + rep / decay
        - 6.0 * disp / rc**7
    )
    u = qq * math.erfc(x) / rc + rep - disp / rc**6
    return dict(
        qq=qq, lead=math.log2(amp), rate=LOG2E / decay, disp=disp, edge=f, base=-u - rc * f
    )


KINDS = [
    kind_constants(7895.4, 0.1709, 29.06, 1.0),
    kind_constants(2314.7, 0.2903, 0.0, -1.0),
    kind_constants(1227.2, 0.3214, 3.47, 1.0),
]
NAMES = ("lead", "rate", "disp", "edge", "base")


def pair_kernel(box, tiles_dev, a_ref, b_ref, pairs_ref, row_ref, col_ref, at_ref, acc_ref, cacc_ref, mi_ref, mf_ref, si_ref, sf_ref, sems):
    blk_i = lax.axis_index("row")
    blk_j = lax.axis_index("col")
    n_first = a_ref.shape[1]
    n_second = b_ref.shape[1]
    wide = n_first <= WIDE_TILES
    entries = pairs_ref.shape[1]
    hi = lax.Precision.HIGHEST
    p = pairs_ref[0:1, :]
    q = pairs_ref[1:2, :]
    pick_a = (lax.broadcasted_iota(jnp.int32, (n_first, entries), 0) == p).astype(jnp.float32)
    pick_b = (lax.broadcasted_iota(jnp.int32, (n_second, entries), 0) == q).astype(jnp.float32)
    tab_a = []
    tab_b = []
    for c in range(4):
        at = a_ref[c].T
        for k in range(0 if wide else at_ref.shape[1]):
            width = min(LANES, n_first - k * LANES)
            at_ref[c, k, :, :width] = at[:, k * LANES : k * LANES + width]
        if c < 3:
            for h in range(2):
                part = at[h * HALF : (h + 1) * HALF]
                tab_a.append(jnp.min(part, 0, keepdims=True))
                tab_a.append(jnp.max(part, 0, keepdims=True))
            bt = b_ref[c].T
            tab_b.append(jnp.min(bt, 0, keepdims=True))
            tab_b.append(jnp.max(bt, 0, keepdims=True))
    fill_a = [jnp.zeros((1, n_first), jnp.float32)] * 4
    fill_b = [jnp.zeros((1, n_second), jnp.float32)] * 2
    got_a = jnp.dot(jnp.concatenate(tab_a + fill_a, 0), pick_a, precision=hi, preferred_element_type=jnp.float32)
    got_b = jnp.dot(jnp.concatenate(tab_b + fill_b, 0), pick_b, precision=hi, preferred_element_type=jnp.float32)
    gaps = [0.0, 0.0]
    plain = p >= 0
    shifts = []
    for c in range(3):
        lows = [got_a[4 * c : 4 * c + 1], got_a[4 * c + 2 : 4 * c + 3]]
        highs = [got_a[4 * c + 1 : 4 * c + 2], got_a[4 * c + 3 : 4 * c + 4]]
        low = jnp.minimum(lows[0], lows[1])
        high = jnp.maximum(highs[0], highs[1])
        blow = got_b[2 * c : 2 * c + 1]
        bhigh = got_b[2 * c + 1 : 2 * c + 2]
        shift = box[c] * jnp.floor(0.5 * (low + high - blow - bhigh) / box[c] + 0.5)
        shifts.append(shift)
        blow = blow + shift
        bhigh = bhigh + shift
        reach = jnp.maximum(high - blow, bhigh - low)
        plain = plain & (reach <= box[c] - cutoff - 0.05)
        for h in range(2):
            gap = jnp.maximum(jnp.maximum(lows[h] - bhigh, blow - highs[h]) - 0.01, 0.0)
            gaps[h] = gaps[h] + gap * gap
    near = [(g < cutoff * cutoff).astype(jnp.int32) for g in gaps]
    same = (p // tiles_dev == blk_j) & (q // tiles_dev == blk_i) & (p % tiles_dev == q % tiles_dev)
    simple = plain & jnp.logical_not(same)
    mode = jnp.where(simple, near[0] + 2 * near[1], jnp.where(same, 8, 4))
    mode = jnp.where(p >= 0, mode, 0)
    mi_ref[0:1, :] = p
    mi_ref[1:2, :] = q
    mi_ref[2:3, :] = mode
    for c in range(3):
        mf_ref[c : c + 1, :] = shifts[c]
    one = pltpu.make_async_copy(mi_ref, si_ref, sems.at[0])
    two = pltpu.make_async_copy(mf_ref, sf_ref, sems.at[1])
    one.start()
    two.start()
    if wide:

        def widen(t, carry):
            for c in range(4):
                at_ref[t, c] = jnp.broadcast_to(a_ref[c, pl.ds(t, 1), :], (TILE, LANES)).T
                acc_ref[t, c] = jnp.zeros((TILE, LANES), jnp.float32)
            return carry

        lax.fori_loop(0, n_first, widen, 0)
    else:
        acc_ref[...] = jnp.zeros_like(acc_ref)
    cacc_ref[...] = jnp.zeros_like(cacc_ref)
    one.wait()
    two.wait()
    lane = lax.broadcasted_iota(jnp.int32, (CHUNK, LANES), 1)
    sub = lax.broadcasted_iota(jnp.int32, (CHUNK, LANES), 0)

    def work(e, half, general):
        first = si_ref[0, e]
        second = si_ref[1, e]
        bank = first // LANES
        spot = first % LANES
        turn = (LANES - spot) % LANES
        rows = [b_ref[c, pl.ds(second, 1), :] for c in range(4)]
        if general:
            mode_now = si_ref[2, e]
            is_same = mode_now >= 8
            weight = jnp.where(is_same, 0.5, 1.0).astype(jnp.float32)
        else:
            for c in range(3):
                rows[c] = rows[c] + sf_ref[c, e]
        spec_b = rows[3] > 0.5
        light = {n: jnp.broadcast_to(jnp.where(spec_b, KINDS[1][n], KINDS[0][n]), (CHUNK, LANES)) for n in NAMES}
        heavy = {n: jnp.broadcast_to(jnp.where(spec_b, KINDS[2][n], KINDS[1][n]), (CHUNK, LANES)) for n in NAMES}
        charge = jnp.broadcast_to(coulomb * (1.0 - 2.0 * rows[3]), (CHUNK, LANES))
        xyz = [jnp.broadcast_to(rows[c], (CHUNK, LANES)) for c in range(3)]
        sums = [jnp.zeros((8, LANES), jnp.float32) for _ in range(4)]
        mine = lane == spot
        starts = range(0, TILE, CHUNK) if general else range(half * HALF, half * HALF + HALF, CHUNK)
        for s in starts:
            cols = [at_ref[first, c, s : s + CHUNK, :] if wide else pltpu.roll(at_ref[c, bank, s : s + CHUNK, :], turn, 1)[:, 0:1] for c in range(4)]
            d = []
            for c in range(3):
                v = cols[c] - xyz[c]
                if general:
                    v = v - box[c] * jnp.floor(v / box[c] + 0.5)
                d.append(v)
            r2 = d[0] * d[0] + d[1] * d[1] + d[2] * d[2]
            inside = r2 < cutoff * cutoff
            if general:
                inside = inside & jnp.logical_not(is_same & (lane == sub + s))
            inv = lax.rsqrt(r2)
            r = r2 * inv
            inv2 = inv * inv
            u = r2 * (1.0 / 72.0) - 1.0
            poly = jnp.float32(SCREEN[-1]) * u + SCREEN[-2]
            for coef in SCREEN[-3::-1]:
                poly = poly * u + coef
            screen = inv - poly
            gauss = jnp.exp2(r2 * (-(alpha_damp**2) * LOG2E) + math.log2(two_over_root * alpha_damp))
            is_cl = jnp.broadcast_to(cols[3], (CHUNK, LANES)) > 0.5
            k = {n: jnp.where(is_cl, heavy[n], light[n]) for n in NAMES}
            qq = jnp.where(is_cl, -charge, charge)
            rep = jnp.exp2(k["lead"] - r * k["rate"])
            six = k["disp"] * (inv2 * inv2 * inv2)
            energy = qq * screen + rep - six + (r * k["edge"] + k["base"])
            over = inv2 * (qq * (screen + gauss) - 6.0 * six) + inv * (
                rep * (k["rate"] * (1.0 / LOG2E)) - k["edge"]
            )
            over = jnp.where(inside, over, 0.0)
            energy = jnp.where(inside, energy, 0.0)
            terms = [over * d[0], over * d[1], over * d[2], energy]
            for c in range(4):
                t = terms[c]
                for m in range(0, CHUNK, 8):
                    sums[c] = sums[c] + t[m : m + 8]
                if wide:
                    acc_ref[first, c, s : s + CHUNK, :] += t * weight if general else t
                    continue
                red = jnp.sum(t, 1, keepdims=True)
                if general:
                    red = red * weight
                acc_ref[c, bank, s : s + CHUNK, :] += jnp.where(mine, red, 0.0)
        for c in range(4):
            v = sums[c]
            if general:
                v = v * weight
            cacc_ref[c, second] += v

    def turn_pair(e, carry):
        mode = si_ref[2, e]
        for half in range(2):
            @pl.when((mode == 1 + half) | (mode == 3))
            def _():
                work(e, half, False)

        @pl.when(mode >= 4)
        def _():
            work(e, 0, True)

        return carry

    lax.fori_loop(0, entries, turn_pair, 0)
    if wide:

        def narrow(t, carry):
            for c in range(4):
                line = jnp.sum(acc_ref[t, c].T, 0, keepdims=True)
                row_ref[c, pl.ds(t, 1), :] = line * (0.5 if c == 3 else 1.0)
            return carry

        lax.fori_loop(0, n_first, narrow, 0)
    for c in range(4):
        scale = 0.5 if c == 3 else 1.0
        for k in range(0 if wide else at_ref.shape[1]):
            width = min(LANES, n_first - k * LANES)
            row_ref[c, k * LANES : k * LANES + width, :] = scale * acc_ref[c, k].T[:width]
        col_ref[c] = jnp.sum(cacc_ref[c], 1) * (0.5 if c == 3 else -1.0)


def reduce_kernel(n_row, n_col, row_ref, col_ref, out_ref, row_got, col_got, send_a, recv_a, send_b, recv_b):
    blk_i = lax.axis_index("row")
    blk_j = lax.axis_index("col")
    tiles = out_ref.shape[1]
    barrier = pltpu.get_barrier_semaphore()
    for k in range(1, n_row):
        pl.semaphore_signal(barrier, inc=1, device_id=(lax.rem(blk_i + k, n_row), blk_j), device_id_type=MESH)
    for k in range(1, n_col):
        pl.semaphore_signal(barrier, inc=1, device_id=(blk_i, lax.rem(blk_j + k, n_col)), device_id_type=MESH)
    pl.semaphore_wait(barrier, n_row + n_col - 2)
    copies = []
    for k in range(1, n_row):
        to = lax.rem(blk_i + k, n_row)
        copies.append(
            pltpu.make_async_remote_copy(
                src_ref=col_ref.at[:, pl.ds(pl.multiple_of(to * tiles, tiles), tiles), :],
                dst_ref=col_got.at[k - 1],
                send_sem=send_b.at[k - 1],
                recv_sem=recv_b.at[k - 1],
                device_id=(to, blk_j),
                device_id_type=MESH,
            )
        )
        copies[-1].start()
    for k in range(1, n_col):
        to = lax.rem(blk_j + k, n_col)
        copies.append(
            pltpu.make_async_remote_copy(
                src_ref=row_ref.at[:, pl.ds(pl.multiple_of(to * tiles, tiles), tiles), :],
                dst_ref=row_got.at[k - 1],
                send_sem=send_a.at[k - 1],
                recv_sem=recv_a.at[k - 1],
                device_id=(blk_i, to),
                device_id_type=MESH,
            )
        )
        copies[-1].start()
    total = row_ref[:, pl.ds(pl.multiple_of(blk_j * tiles, tiles), tiles), :] + col_ref[:, pl.ds(pl.multiple_of(blk_i * tiles, tiles), tiles), :]
    for copy in copies:
        copy.wait()
    for k in range(n_row - 1):
        total = total + col_got[k]
    for k in range(n_col - 1):
        total = total + row_got[k]
    out_ref[...] = total


def exchange_kernel(n_row, n_col, pos_ref, spec_ref, dest_ref, a_ref, b_ref, outgoing, arrived, owned, send_x, recv_x, send_a, recv_a, send_b, recv_b):
    blk_i = lax.axis_index("row")
    blk_j = lax.axis_index("col")
    owners = n_row * n_col
    me = blk_i * n_col + blk_j
    tiles = owned.shape[1]
    atoms = pos_ref.shape[1]
    capacity = atoms // owners
    ratio = TILE // capacity
    barrier = pltpu.get_barrier_semaphore()

    def coords(k):
        to = lax.rem(me + k, owners)
        return to, (to // n_col, lax.rem(to, n_col))

    def greet(k, carry):
        pl.semaphore_signal(barrier, inc=1, device_id=coords(k)[1], device_id_type=MESH)
        return carry

    lax.fori_loop(1, owners, greet, 0)
    owner_hot = lax.broadcasted_iota(jnp.int32, (owners, atoms), 0) == dest_ref[0:1, :]
    lane = lax.rem(dest_ref[1:2, :], capacity) + lax.rem(me, ratio) * capacity
    lane_hot = (lax.broadcasted_iota(jnp.int32, (TILE, atoms), 0) == lane).astype(jnp.float32).astype(jnp.bfloat16)
    for c in range(4):
        rest = pos_ref[c : c + 1, :] if c < 3 else spec_ref[...].astype(jnp.float32)
        total = None
        for piece in range(3 if c < 3 else 1):
            part = rest.astype(jnp.bfloat16).astype(jnp.float32)
            rest = rest - part
            spread = jnp.where(owner_hot, part, 0.0).astype(jnp.bfloat16)
            got = lax.dot_general(spread, lane_hot, (((1,), (1,)), ((), ())), preferred_element_type=jnp.float32)
            total = got if total is None else total + got
        outgoing[:, c, :] = total
    pl.semaphore_wait(barrier, owners - 1)

    def send(k):
        to, where = coords(k)
        return pltpu.make_async_remote_copy(
            src_ref=outgoing.at[to],
            dst_ref=arrived.at[me],
            send_sem=send_x.at[k - 1],
            recv_sem=recv_x.at[k - 1],
            device_id=where,
            device_id_type=MESH,
        )

    def start(k, carry):
        send(k).start()
        return carry

    def finish(k, carry):
        send(k).wait()
        return carry

    lax.fori_loop(1, owners, start, 0)
    arrived[pl.ds(me, 1)] = outgoing[pl.ds(me, 1)]
    lax.fori_loop(1, owners, finish, 0)
    whole = jnp.sum(arrived[...].reshape(tiles, ratio, 4, TILE), 1)
    for c in range(4):
        owned[c] = whole[:, c, :]
    copies = []
    at_a = pl.ds(pl.multiple_of(blk_j * tiles, tiles), tiles)
    at_b = pl.ds(pl.multiple_of(blk_i * tiles, tiles), tiles)
    for k in range(1, n_row):
        copies.append(
            pltpu.make_async_remote_copy(
                src_ref=owned,
                dst_ref=b_ref.at[:, at_b, :],
                send_sem=send_b.at[k - 1],
                recv_sem=recv_b.at[k - 1],
                device_id=(lax.rem(blk_i + k, n_row), blk_j),
                device_id_type=MESH,
            )
        )
        copies[-1].start()
    for k in range(1, n_col):
        copies.append(
            pltpu.make_async_remote_copy(
                src_ref=owned,
                dst_ref=a_ref.at[:, at_a, :],
                send_sem=send_a.at[k - 1],
                recv_sem=recv_a.at[k - 1],
                device_id=(blk_i, lax.rem(blk_j + k, n_col)),
                device_id_type=MESH,
            )
        )
        copies[-1].start()
    a_ref[:, at_a, :] = owned[...]
    b_ref[:, at_b, :] = owned[...]
    for copy in copies:
        copy.wait()


def local(positions, species, destination, pair_tiles):
    n_row = lax.axis_size("row")
    n_col = lax.axis_size("col")
    atom_dev = positions.shape[1]
    owners = n_row * n_col
    tiles_dev = atom_dev // TILE
    n_first = n_col * tiles_dev
    n_second = n_row * tiles_dev
    vmem = pl.BlockSpec(memory_space=pltpu.VMEM)
    row_block, col_block = pl.pallas_call(
        functools.partial(exchange_kernel, n_row, n_col),
        out_shape=(
            jax.ShapeDtypeStruct((4, n_first, TILE), jnp.float32),
            jax.ShapeDtypeStruct((4, n_second, TILE), jnp.float32),
        ),
        in_specs=[vmem] * 3,
        out_specs=(vmem, vmem),
        scratch_shapes=[
            pltpu.VMEM((owners, 4, TILE), jnp.float32),
            pltpu.VMEM((owners, 4, TILE), jnp.float32),
            pltpu.VMEM((4, tiles_dev, TILE), jnp.float32),
            pltpu.SemaphoreType.DMA((owners - 1,)),
            pltpu.SemaphoreType.DMA((owners - 1,)),
            pltpu.SemaphoreType.DMA((n_col - 1,)),
            pltpu.SemaphoreType.DMA((n_col - 1,)),
            pltpu.SemaphoreType.DMA((n_row - 1,)),
            pltpu.SemaphoreType.DMA((n_row - 1,)),
        ],
        compiler_params=pltpu.CompilerParams(
            collective_id=1, has_side_effects=True, vmem_limit_bytes=40 * 1024 * 1024
        ),
        name="exchange",
    )(positions, species[None], destination)
    box = (4 * lattice * n_row, 4 * lattice * n_col, 8 * lattice * tiles_dev)
    entries = pair_tiles.shape[3]
    lists = pair_tiles.reshape(2, entries)
    banks = -(-n_first // LANES)
    side = (n_first, 4, TILE, LANES) if n_first <= WIDE_TILES else (4, banks, TILE, LANES)
    row_part, col_part = pl.pallas_call(
        functools.partial(pair_kernel, box, tiles_dev),
        out_shape=(
            jax.ShapeDtypeStruct((4, n_first, TILE), jnp.float32),
            jax.ShapeDtypeStruct((4, n_second, TILE), jnp.float32),
        ),
        in_specs=[vmem] * 3,
        out_specs=(vmem, vmem),
        scratch_shapes=[
            pltpu.VMEM(side, jnp.float32),
            pltpu.VMEM(side, jnp.float32),
            pltpu.VMEM((4, n_second, 8, LANES), jnp.float32),
            pltpu.VMEM((8, entries), jnp.int32),
            pltpu.VMEM((8, entries), jnp.float32),
            pltpu.SMEM((8, entries), jnp.int32),
            pltpu.SMEM((8, entries), jnp.float32),
            pltpu.SemaphoreType.DMA((2,)),
        ],
        compiler_params=pltpu.CompilerParams(vmem_limit_bytes=48 * 1024 * 1024),
        name="pairs",
    )(row_block, col_block, lists)
    out = pl.pallas_call(
        functools.partial(reduce_kernel, n_row, n_col),
        out_shape=jax.ShapeDtypeStruct((4, tiles_dev, TILE), jnp.float32),
        in_specs=[vmem] * 2,
        out_specs=vmem,
        scratch_shapes=[
            pltpu.VMEM((n_col - 1, 4, tiles_dev, TILE), jnp.float32),
            pltpu.VMEM((n_row - 1, 4, tiles_dev, TILE), jnp.float32),
            pltpu.SemaphoreType.DMA((n_col - 1,)),
            pltpu.SemaphoreType.DMA((n_col - 1,)),
            pltpu.SemaphoreType.DMA((n_row - 1,)),
            pltpu.SemaphoreType.DMA((n_row - 1,)),
        ],
        compiler_params=pltpu.CompilerParams(
            collective_id=0, has_side_effects=True, vmem_limit_bytes=32 * 1024 * 1024
        ),
        name="reduce",
    )(row_part, col_part)
    return out.reshape(4, atom_dev)


def solution(mesh):
    return jax.shard_map(
        local,
        mesh=mesh,
        in_specs=(
            P(None, ("row", "col")),
            P(("row", "col")),
            P(None, ("row", "col")),
            P("row", "col", None, None),
        ),
        out_specs=P(None, ("row", "col")),
        check_vma=False,
    )
```
